256 devices in a mesh: blk: 128 (over x, z, y_lo, core), rep: 2 (over y_hi).
Axes of the slice: x: 4, y: 4 (y_hi: 2, y_lo: 2; y = y_hi * 2 + y_lo), z: 8, core: 2. Of those that a mesh axis runs over, the one named last changes fastest.
Arguments:
- images: bfloat16 [196608, 1152], P(('rep', 'blk')), parts along dimension 0, may hold values from -0.1875 to 0.1875
- texts: bfloat16 [196608, 1152], P(('rep', 'blk')), parts along dimension 0, may hold values from -0.1875 to 0.1875
- positive: int32 [196608], P(('rep', 'blk')), parts along dimension 0, may hold values from 0 to 98303, as said below
- log_scale: float32 [2], P('rep'), parts along dimension 0, may hold values from 1.5 to 2.5
- bias: float32 [2], P('rep'), parts along dimension 0, may hold values from -4 to -2
Outputs:
- row_loss: float32 [196608], P(('rep', 'blk')), parts along dimension 0
- grad_image: float32 [196608, 1152], P(('rep', 'blk')), parts along dimension 0
- grad_text: float32 [196608, 1152], P(('rep', 'blk')), parts along dimension 0
The draws below stay inside these ranges and needn't reach their ends.
There are 2 independent parts, one for each index of `rep`. The reference program is written for one: setup_inputs(seed, part) draws one part's arguments, and reference() takes and returns one part's arrays. A program takes and returns all parts, laid end to end along the dimension named above; each array names one. Nothing has to cross between parts.
Inputs may be any that keep to these rules, and one draw needn't show every extreme that they name: The positive text row of an image row of block k lies in one of the 3 text blocks k, k-1, ..., counted backwards around the 128 blocks.
All inputs are finite; a program needn't handle non-finite values.
Results may differ from the reference program's by a relative error of at most 0.0042.
Values may be sent and summed in bfloat16 or wider, within the bound.
A program may use at most 64 MiB of HBM per device.

```python
import jax
import jax.numpy as jnp
from jax import lax

D = 1152
ROWS = 768
STEPS = 3
TOTAL = 98304


def draw_positive(key, part):
    key = jax.random.fold_in(key, 5)
    first_key, second_key = jax.random.split(key)
    block_count = TOTAL // ROWS
    owners = jnp.arange(TOTAL, dtype=jnp.int32) // ROWS
    backward = jax.random.randint(first_key, (TOTAL,), 0, STEPS, dtype=jnp.int32)
    within = jax.random.randint(second_key, (TOTAL,), 0, ROWS, dtype=jnp.int32)
    backward = backward.at[0].set(0).at[TOTAL - 1].set(0)
    within = within.at[0].set(0).at[TOTAL - 1].set(ROWS - 1)
    return (owners - backward) % block_count * ROWS + within


def shard_levels(rng, shape, shards, low, largest):
    def one(axis_at, parts):
        draws = jax.random.uniform(jax.random.fold_in(jax.random.fold_in(rng, 6), axis_at), (parts,), jnp.float32, low / len(shards), largest / len(shards))
        return jnp.repeat(jnp.exp(draws), shape[axis_at] // parts).reshape((-1,) + (1,) * (len(shape) - axis_at - 1))

    level = one(*shards[0])
    for cut in shards[1:]:
        level = level * one(*cut)
    return level


def scatter_about(key, extent, scale, reach, cuts=(), kind=jnp.bfloat16):
    result = jax.random.normal(key, extent, jnp.float32) * scale
    if len(cuts) > 0:
        result = shard_levels(key, extent, cuts, -0.22, 0.18) * result
    return jnp.clip(result, min=-reach, max=reach).astype(kind)


def setup_inputs(seed: int = 0, part: int = 0) -> dict:
    seeds = jax.random.split(jax.random.key(seed), 6)
    part_keys = jax.random.split(jax.random.fold_in(seeds[5], part), 6)
    return {
        "images": scatter_about(part_keys[0], (TOTAL, D), D ** -0.5, 0.1875, ((0, 128),)),
        "texts": scatter_about(part_keys[1], (TOTAL, D), D ** -0.5, 0.1875, ((0, 128),)),
        "positive": draw_positive(jax.random.fold_in(jax.random.fold_in(seeds[5], part), 71), part),
        "log_scale": jnp.clip(jax.random.uniform(part_keys[3], (1,), jnp.float32, 1.5, 2.5), 1.5, 2.5),
        "bias": jnp.clip(jax.random.uniform(part_keys[4], (1,), jnp.float32, -4.0, -2.0), -4.0, -2.0),
    }


def normalize(values):
    wide = values.astype(jnp.float32)
    inverse = lax.rsqrt(lax.optimization_barrier(jnp.sum(wide * wide, axis=-1, keepdims=True)) + 1e-06)
    return (wide * inverse, inverse)

def reference(images, texts, positive, log_scale, bias):
    x_unit, x_inv = normalize(images)
    y_unit, y_inv = normalize(texts)
    block_count = TOTAL // ROWS
    x_blocks = x_unit.astype(jnp.bfloat16).astype(jnp.float32).reshape(block_count, ROWS, D)
    y_blocks = y_unit.astype(jnp.bfloat16).astype(jnp.float32).reshape(block_count, ROWS, D)
    pairs = positive.reshape(block_count, ROWS).astype(jnp.int32)
    logit_scale = jnp.exp(log_scale[0])
    logit_bias = bias[0]
    block_ids = jnp.arange(block_count).astype(jnp.int32)
    columns = jnp.arange(ROWS).astype(jnp.int32)
    loss_sum = jnp.zeros((block_count, ROWS), jnp.float32)
    grad_x = jnp.zeros((block_count, ROWS, D), jnp.float32)
    grad_y = jnp.zeros((block_count, ROWS, D), jnp.float32)
    for turn_index in range(STEPS):
        rolled = jnp.roll(y_blocks, turn_index, axis=0)
        source = (block_ids - turn_index) % block_count
        target = (source[:, None, None] * ROWS + columns[None, None, :]).astype(jnp.int32)
        labels = jnp.where(pairs[:, :, None] == target, 1.0, -1.0).astype(jnp.float32)
        logits = jnp.einsum('krd,kcd->krc', x_blocks, rolled, precision=lax.Precision.HIGHEST)
        scaled = logit_scale * logits + logit_bias
        loss_sum = loss_sum + lax.optimization_barrier(jnp.sum(jax.nn.softplus(-labels * scaled), axis=-1))
        coefficient = (-labels * jax.nn.sigmoid(-labels * scaled)).astype(jnp.bfloat16).astype(jnp.float32)
        grad_x = grad_x + logit_scale * jnp.einsum('krc,kcd->krd', coefficient, rolled, precision=lax.Precision.HIGHEST)
        text_term = logit_scale * jnp.einsum('krc,krd->kcd', coefficient, x_blocks, precision=lax.Precision.HIGHEST)
        grad_y = grad_y + jnp.roll(text_term, -turn_index, axis=0)
    grad_x = grad_x.reshape(TOTAL, D)
    grad_y = grad_y.reshape(TOTAL, D)
    grad_image = (grad_x - x_unit * lax.optimization_barrier(jnp.sum(x_unit * grad_x, axis=-1, keepdims=True))) * x_inv
    grad_text = (grad_y - y_unit * lax.optimization_barrier(jnp.sum(y_unit * grad_y, axis=-1, keepdims=True))) * y_inv
    row_loss = loss_sum.reshape(TOTAL) / ROWS
    return (row_loss, grad_image, grad_text)
```

```python
import functools

import jax
import jax.numpy as jnp
from jax import lax
from jax.experimental import pallas as pl
from jax.experimental.pallas import tpu as pltpu
from jax.sharding import PartitionSpec as P

STEPS = 3
CHUNK = 128
MESH = pl.DeviceIdType.MESH


def kernel(
    scale_ref, bias_ref, pos_ref, img_ref, txt_ref,
    loss_ref, gx_ref, gy_ref,
    xraw, yraw, xl, yl, xinv, yinv, t1, t2, i1, i2, pos1, pos2, posb, loss_acc,
    load_sem, link_t_s, link_t_r, link_i_s, link_i_r, d2d_t_s, d2d_t_r, d2d_i_s, d2d_i_r,
    pos_s, pos_r,
):
    rows, width = xraw.shape
    chunks = rows // CHUNK
    n = lax.axis_size("blk")
    me = lax.axis_index("blk")
    core = lax.rem(me, 2)
    ahead = lax.rem(me + 2, n)
    behind = lax.rem(me + n - 2, n)
    partner = me + 1 - 2 * core
    first = core == 0
    second = core == 1

    barrier = pltpu.get_barrier_semaphore()
    for other in (ahead, behind, partner):
        pl.semaphore_signal(barrier, inc=1, device_id={"blk": other}, device_id_type=MESH)

    def part(c):
        return pl.ds(pl.multiple_of(c * CHUNK, CHUNK), CHUNK)

    load_x = pltpu.make_async_copy(img_ref, xraw, load_sem.at[0])
    load_y = pltpu.make_async_copy(txt_ref, yraw, load_sem.at[1])
    load_y.start()
    load_x.start()

    def normalize(raw, low, inv):
        def step(c, carry):
            wide = raw[part(c), :].astype(jnp.float32)
            inverse = lax.rsqrt(jnp.sum(wide * wide, axis=-1, keepdims=True) + 1e-06)
            inv[part(c), :] = jnp.broadcast_to(inverse, (CHUNK, 128))
            low[part(c), :] = (wide * inverse).astype(jnp.bfloat16)
            return carry

        lax.fori_loop(0, chunks, step, 0)

    load_y.wait()
    normalize(yraw, yl, yinv)
    load_x.wait()
    normalize(xraw, xl, xinv)

    def link_t(c):
        return pltpu.make_async_remote_copy(
            src_ref=yl.at[part(c)], dst_ref=t2.at[part(c)], send_sem=link_t_s.at[c], recv_sem=link_t_r.at[c],
            device_id={"blk": ahead}, device_id_type=MESH)

    def link_i(c):
        return pltpu.make_async_remote_copy(
            src_ref=xl.at[part(c)], dst_ref=i2.at[part(c)], send_sem=link_i_s.at[c], recv_sem=link_i_r.at[c],
            device_id={"blk": behind}, device_id_type=MESH)

    def d2d_t(c, source):
        return pltpu.make_async_remote_copy(
            src_ref=source.at[part(c)], dst_ref=t1.at[part(c)], send_sem=d2d_t_s.at[c], recv_sem=d2d_t_r.at[c],
            device_id={"blk": partner}, device_id_type=MESH)

    def d2d_i(c, source):
        return pltpu.make_async_remote_copy(
            src_ref=source.at[part(c)], dst_ref=i1.at[part(c)], send_sem=d2d_i_s.at[c], recv_sem=d2d_i_r.at[c],
            device_id={"blk": partner}, device_id_type=MESH)

    pos_link = pltpu.make_async_remote_copy(
        src_ref=pos_ref, dst_ref=pos2, send_sem=pos_s.at[0], recv_sem=pos_r.at[0],
        device_id={"blk": behind}, device_id_type=MESH)

    def pos_d2d(source):
        return pltpu.make_async_remote_copy(
            src_ref=source, dst_ref=pos1, send_sem=pos_s.at[1], recv_sem=pos_r.at[1],
            device_id={"blk": partner}, device_id_type=MESH)

    pl.semaphore_wait(barrier, 3)
    pos_link.start()

    def start_t(c, carry):
        link_t(c).start()
        return carry

    def start_i(c, carry):
        link_i(c).start()
        return carry

    lax.fori_loop(0, chunks, start_t, 0)
    lax.fori_loop(0, chunks, start_i, 0)

    @pl.when(first)
    def _():
        def go(c, carry):
            d2d_t(c, yl).start()
            return carry

        lax.fori_loop(0, chunks, go, 0)

    @pl.when(second)
    def _():
        pos_d2d(pos_ref).start()

        def go(c, carry):
            d2d_i(c, xl).start()
            return carry

        lax.fori_loop(0, chunks, go, 0)

    scale = jnp.exp(jnp.full((8, 128), scale_ref[0], jnp.float32))[0:1]
    bias = jnp.full((1, 128), bias_ref[0], jnp.float32)
    gx_ref[...] = jnp.zeros_like(gx_ref)
    gy_ref[...] = jnp.zeros_like(gy_ref)
    loss_acc[...] = jnp.zeros_like(loss_acc)

    def spread(c, carry):
        row = pos_ref[pl.ds(c, 1), :].astype(jnp.float32)
        posb[part(c), :] = jnp.broadcast_to(row, (CHUNK, CHUNK)).T
        return carry

    lax.fori_loop(0, chunks, spread, 0)

    lanes = lax.broadcasted_iota(jnp.int32, (CHUNK, CHUNK), 1)
    subs = lax.broadcasted_iota(jnp.int32, (CHUNK, CHUNK), 0)

    def text_chunk(block, source, c):
        base = (source * rows + c * CHUNK + lanes).astype(jnp.float32)

        def tile(r, carry):
            logits = lax.dot_general(
                xl[part(r), :], block[part(c), :], (((1,), (1,)), ((), ())), preferred_element_type=jnp.float32)
            scaled = scale * logits + bias
            match = posb[part(r), :] == base
            z = jnp.where(match, -scaled, scaled)
            e = jnp.exp(-jnp.abs(z))
            loss_acc[part(r), :] += jnp.maximum(z, 0.0) + jnp.log1p(e)
            s = jnp.where(z >= 0, 1.0, e) / (1.0 + e)
            coefficient = jnp.where(match, -s, s).astype(jnp.bfloat16)
            gx_ref[part(r), :] += jnp.dot(coefficient, block[part(c), :], preferred_element_type=jnp.float32)
            return carry

        lax.fori_loop(0, chunks, tile, 0)

    def image_chunk(block, positions, c):
        pos_row = positions[pl.ds(c, 1), :]

        def tile(r, carry):
            logits = lax.dot_general(
                yl[part(r), :], block[part(c), :], (((1,), (1,)), ((), ())), preferred_element_type=jnp.float32)
            scaled = scale * logits + bias
            match = pos_row == (me * rows + r * CHUNK + subs)
            z = jnp.where(match, -scaled, scaled)
            s = 1.0 / (1.0 + jnp.exp(-z))
            coefficient = jnp.where(match, -s, s).astype(jnp.bfloat16)
            gy_ref[part(r), :] += jnp.dot(coefficient, block[part(c), :], preferred_element_type=jnp.float32)
            return carry

        lax.fori_loop(0, chunks, tile, 0)

    def own(c, carry):
        text_chunk(yl, me, c)
        image_chunk(xl, pos_ref, c)
        return carry

    lax.fori_loop(0, chunks, own, 0)

    def texts_in(c, carry):
        link_t(c).wait_recv()

        @pl.when(second)
        def _():
            d2d_t(c, t2).start()

        text_chunk(t2, lax.rem(me + n - 2, n), c)
        d2d_t(c, yl).wait_recv()
        text_chunk(t1, lax.rem(me + n - 1, n), c)
        return carry

    lax.fori_loop(0, chunks, texts_in, 0)

    def finish(acc, raw, inv):
        def step(c, carry):
            unit = raw[part(c), :].astype(jnp.float32) * inv[part(c), 0:1]
            grad = acc[part(c), :] * scale[0:1, 0:1]
            dot = jnp.sum(unit * grad, axis=-1, keepdims=True)
            acc[part(c), :] = (grad - unit * dot) * inv[part(c), 0:1]
            return carry

        lax.fori_loop(0, chunks, step, 0)

    finish(gx_ref, xraw, xinv)

    def losses(c, carry):
        total = jnp.sum(loss_acc[part(c), :].T, axis=0, keepdims=True)
        loss_ref[pl.ds(c, 1), :] = total / rows
        return carry

    lax.fori_loop(0, chunks, losses, 0)

    pos_link.wait_recv()

    @pl.when(first)
    def _():
        pos_d2d(pos2).start()

    def images_in(c, carry):
        link_i(c).wait_recv()

        @pl.when(first)
        def _():
            d2d_i(c, i2).start()

        image_chunk(i2, pos2, c)

        @pl.when(c == 0)
        def _():
            pos_d2d(pos_ref).wait_recv()

        d2d_i(c, xl).wait_recv()
        image_chunk(i1, pos1, c)
        return carry

    lax.fori_loop(0, chunks, images_in, 0)
    finish(gy_ref, yraw, yinv)

    pos_link.wait_send()
    pos_d2d(pos_ref).wait_send()

    def drain(c, carry):
        link_t(c).wait_send()
        link_i(c).wait_send()
        d2d_t(c, yl).wait_send()
        d2d_i(c, xl).wait_send()
        return carry

    lax.fori_loop(0, chunks, drain, 0)


def shards(images, texts, positive, log_scale, bias):
    rows, width = images.shape
    chunks = rows // CHUNK
    low = pltpu.VMEM((rows, width), jnp.bfloat16)
    column = pltpu.VMEM((rows, 128), jnp.float32)
    places = pltpu.VMEM((chunks, CHUNK), jnp.int32)
    sems = pltpu.SemaphoreType.DMA((chunks,))
    pair = pltpu.SemaphoreType.DMA((2,))
    vmem = pl.BlockSpec(memory_space=pltpu.VMEM)
    smem = pl.BlockSpec(memory_space=pltpu.SMEM)
    hbm = pl.BlockSpec(memory_space=pl.ANY)
    loss, grad_x, grad_y = pl.pallas_call(
        kernel,
        out_shape=(
            jax.ShapeDtypeStruct((chunks, CHUNK), jnp.float32),
            pltpu.VMEM((rows, width), jnp.float32),
            pltpu.VMEM((rows, width), jnp.float32),
        ),
        in_specs=[smem, smem, vmem, hbm, hbm],
        out_specs=(vmem, vmem, vmem),
        scratch_shapes=[low] * 4 + [column] * 2 + [low] * 4 + [places] * 2 + [column] * 2 + [pair] + [sems] * 8 + [pair] * 2,
        compiler_params=pltpu.CompilerParams(
            collective_id=0, has_side_effects=True, vmem_limit_bytes=40 * 2**20),
    )(log_scale, bias, positive.reshape(chunks, CHUNK), images, texts)
    return (loss.reshape(rows), grad_x, grad_y)


def solution(mesh):
    in_specs = (
        P(("rep", "blk"), None),
        P(("rep", "blk"), None),
        P(("rep", "blk")),
        P("rep"),
        P("rep"),
    )
    out_specs = (P(("rep", "blk")), P(("rep", "blk"), None), P(("rep", "blk"), None))
    return jax.shard_map(shards, mesh=mesh, in_specs=in_specs, out_specs=out_specs, check_vma=False)
```

```python
import functools

import jax
import jax.numpy as jnp
from jax import lax
from jax.experimental import pallas as pl
from jax.experimental.pallas import tpu as pltpu
from jax.sharding import PartitionSpec as P

PART = 128
TILE = 256
LAST_TILE = 256
IN_FLIGHT = 4
MESH = pl.DeviceIdType.MESH
IMAGE, TEXT = 0, 1
FAR, NEAR = 0, 1


def at_rows(start, size):
    return pl.ds(pl.multiple_of(start, size), size)


def kernel(
    scale_hbm, bias_hbm, pos_hbm, img_ref, txt_ref,
    loss_ref, gx_ref, gy_ref,
    scale_ref, bias_ref, pos_ref, raw, low, inv, there, places, posb, loss_acc,
    load_sem, lead_s, lead_r, tail_s, tail_r, pass_s, pass_r, whole_s, whole_r, pos_s, pos_r,
):
    _, rows, width = raw.shape
    parts = rows // PART
    tiles = rows // TILE
    n = lax.axis_size("blk")
    me = lax.axis_index("blk")
    core = lax.rem(me, 2)
    other = 1 - core
    ahead = lax.rem(me + 2, n)
    behind = lax.rem(me + n - 2, n)
    partner = me + 1 - 2 * core
    first = core == 0
    second = core == 1

    barrier = pltpu.get_barrier_semaphore()
    for device in (ahead, behind, partner):
        pl.semaphore_signal(barrier, inc=1, device_id={"blk": device}, device_id_type=MESH)

    loads = [
        pltpu.make_async_copy(img_ref, raw.at[IMAGE], load_sem.at[0]),
        pltpu.make_async_copy(txt_ref, raw.at[TEXT], load_sem.at[1]),
        pltpu.make_async_copy(pos_hbm, pos_ref, load_sem.at[2]),
        pltpu.make_async_copy(scale_hbm, scale_ref, load_sem.at[3]),
        pltpu.make_async_copy(bias_hbm, bias_ref, load_sem.at[4]),
    ]
    for load in loads:
        load.start()

    def remote(source, target, sent, got, device):
        return pltpu.make_async_remote_copy(
            src_ref=source, dst_ref=target, send_sem=sent, recv_sem=got,
            device_id={"blk": device}, device_id_type=MESH)

    def lead(c):
        r = at_rows(c * PART, PART)
        return remote(low.at[core, r], there.at[core, FAR, r], lead_s.at[c], lead_r.at[c],
                      jnp.where(first, behind, ahead))

    def tail(c):
        r = at_rows(c * PART, PART)
        return remote(low.at[other, r], there.at[other, FAR, r], tail_s.at[c], tail_r.at[c],
                      jnp.where(first, ahead, behind))

    def pass_on(c):
        r = at_rows(c * PART, PART)
        return remote(there.at[core, FAR, r], there.at[core, NEAR, r], pass_s.at[c], pass_r.at[c], partner)

    whole = remote(low.at[other], there.at[other, NEAR], whole_s.at[0], whole_r.at[0], partner)
    pos_link = remote(pos_ref, places.at[FAR], pos_s.at[0], pos_r.at[0], behind)

    def pos_near(source):
        return remote(source, places.at[NEAR], pos_s.at[1], pos_r.at[1], partner)

    def normalize(kind):
        def step(c, carry):
            r = at_rows(c * PART, PART)
            wide = raw[kind, r, :].astype(jnp.float32)
            inverse = lax.rsqrt(jnp.sum(wide * wide, axis=-1, keepdims=True) + 1e-06)
            inv[kind, r, :] = jnp.broadcast_to(inverse, (PART, 128))
            low[kind, r, :] = (wide * inverse).astype(jnp.bfloat16)
            return carry

        lax.fori_loop(0, parts, step, 0)

    loads[0].wait()
    normalize(IMAGE)
    loads[1].wait()
    normalize(TEXT)
    for load in loads[2:]:
        load.wait()

    pl.semaphore_wait(barrier, 3)
    def start(p):
        is_tail = jnp.logical_or(p == 2 * parts - 1, jnp.logical_and(p > 0, lax.rem(p, 2) == 0))

        @pl.when(jnp.logical_and(p < 2 * parts, is_tail))
        def _():
            tail(lax.div(p - 1, 2)).start()

        @pl.when(jnp.logical_and(p < 2 * parts, jnp.logical_not(is_tail)))
        def _():
            lead(lax.div(p + 1, 2)).start()

    def fill(p, carry):
        start(p)
        return carry

    pos_link.start()

    @pl.when(second)
    def _():
        pos_near(pos_ref).start()

    whole.start()
    lax.fori_loop(0, IN_FLIGHT, fill, 0)

    scale = jnp.exp(jnp.full((8, 128), scale_ref[0], jnp.float32))[0:1, 0:1]
    bias = bias_ref[0]

    def spread(c, carry):
        row = pos_ref[pl.ds(c, 1), :].astype(jnp.float32)
        posb[at_rows(c * 128, 128), :] = jnp.broadcast_to(row, (128, 128)).T
        return carry

    lax.fori_loop(0, rows // 128, spread, 0)

    def logits_of(own, block):
        dots = lax.dot_general(own, block, (((1,), (1,)), ((), ())), preferred_element_type=jnp.float32)
        return scale * dots + bias

    def text_terms(at, block, target, wide):
        scaled = logits_of(low[IMAGE, at, :], block)
        match = jnp.concatenate([posb[at, :]] * (wide // 128), axis=1) == target
        z = jnp.where(match, -scaled, scaled)
        e = jnp.exp(-jnp.abs(z))
        term = jnp.maximum(z, 0.0) + jnp.log1p(e)
        s = jnp.where(z >= 0, 1.0, e) / (1.0 + e)
        coefficient = jnp.where(match, -s, s).astype(jnp.bfloat16)
        loss = functools.reduce(jnp.add, [term[:, g:g + 128] for g in range(0, wide, 128)])
        return loss, jnp.dot(coefficient, block, preferred_element_type=jnp.float32)

    def image_terms(at, start, size, block, pos_row):
        scaled = logits_of(low[TEXT, at, :], block)
        subs = lax.broadcasted_iota(jnp.int32, scaled.shape, 0)
        match = pos_row == me * rows + start + subs
        z = jnp.where(match, -scaled, scaled)
        s = 1.0 / (1.0 + jnp.exp(-z))
        coefficient = jnp.where(match, -s, s).astype(jnp.bfloat16)
        return jnp.dot(coefficient, block, preferred_element_type=jnp.float32)

    def targets(source, start, size, wide):
        lanes = lax.broadcasted_iota(jnp.int32, (size, wide), 1)
        return (source * rows + start + lanes).astype(jnp.float32)

    def text_whole(block, source, fresh):
        def step(t, carry):
            at = at_rows(t * TILE, TILE)
            loss, grad = text_terms(at, block[...], targets(source, 0, TILE, rows), rows)
            loss_acc[at, :] = loss if fresh else loss_acc[at, :] + loss
            gx_ref[at, :] = grad if fresh else gx_ref[at, :] + grad
            return carry

        lax.fori_loop(0, tiles, step, 0)

    def image_whole(block, positions, fresh):
        pos_row = jnp.concatenate([positions[g:g + 1, :] for g in range(rows // 128)], axis=1)

        def step(t, carry):
            at = at_rows(t * TILE, TILE)
            grad = image_terms(at, t * TILE, TILE, block[...], pos_row)
            gy_ref[at, :] = grad if fresh else gy_ref[at, :] + grad
            return carry

        lax.fori_loop(0, tiles, step, 0)

    def project(grad, kind, at):
        inverse = inv[kind, at, :][:, 0:1]
        unit = raw[kind, at, :].astype(jnp.float32) * inverse
        grad = grad * scale
        return (grad - unit * jnp.sum(unit * grad, axis=-1, keepdims=True)) * inverse

    def text_part(block, source, c, last=False):
        size = LAST_TILE if last else TILE
        chunk = block[at_rows(c * PART, PART), :]
        for t in range(rows // size):
            at = pl.ds(t * size, size)
            loss, grad = text_terms(at, chunk, targets(source, c * PART, size, PART), PART)
            loss_acc[at, :] += loss
            grad = gx_ref[at, :] + grad
            gx_ref[at, :] = project(grad, IMAGE, at) if last else grad

    def image_part(block, positions, c, last=False):
        size = LAST_TILE if last else TILE
        chunk = block[at_rows(c * PART, PART), :]
        pos_row = positions[pl.ds(c, 1), :]
        for t in range(rows // size):
            at = pl.ds(t * size, size)
            grad = gy_ref[at, :] + image_terms(at, t * size, size, chunk, pos_row)
            gy_ref[at, :] = project(grad, TEXT, at) if last else grad

    def finish(acc, kind):
        def step(t, carry):
            at = at_rows(t * TILE, TILE)
            acc[at, :] = project(acc[at, :], kind, at)
            return carry

        lax.fori_loop(0, tiles, step, 0)

    def losses():
        for c in range(rows // 128):
            total = jnp.sum(loss_acc[c * 128:(c + 1) * 128, :].T, axis=0, keepdims=True)
            loss_ref[c:c + 1, :] = total / rows

    near_text = lax.rem(me + n - 1, n)
    far_text = lax.rem(me + n - 2, n)

    text_whole(low.at[TEXT], me, True)
    image_whole(low.at[IMAGE], pos_ref, True)
    def steps(c, carry):
        lead(c).wait_send()

        start(jnp.where(c == 0, 0, 2 * c - 1) + IN_FLIGHT)
        lead(c).wait_recv()

        @pl.when(c == 0)
        def _():
            pos_link.wait_recv()

            @pl.when(first)
            def _():
                pos_near(places.at[FAR]).start()

            pos_near(pos_ref).wait_recv()

        pass_on(c).start()
        pass_on(c).wait_recv()
        image_part(there.at[IMAGE, core], places.at[core], c)
        text_part(there.at[TEXT, other], jnp.where(first, near_text, far_text), c)

        @pl.when(c > 0)
        def _():
            tail(c - 1).wait_send()
            start(2 * c + IN_FLIGHT)

        @pl.when(jnp.logical_and(c == parts - 1, first))
        def _():
            finish(gy_ref, TEXT)

        @pl.when(jnp.logical_and(c == parts - 1, second))
        def _():
            finish(gx_ref, IMAGE)
            losses()

        @pl.when(c > 0)
        def _():
            tail(c - 1).wait_recv()

            @pl.when(first)
            def _():
                text_part(there.at[TEXT, FAR], far_text, c - 1)

            @pl.when(second)
            def _():
                image_part(there.at[IMAGE, FAR], places.at[FAR], c - 1)

        @pl.when(c == 1)
        def _():
            whole.wait_recv()

            @pl.when(first)
            def _():
                image_whole(there.at[IMAGE, NEAR], places.at[NEAR], False)

            @pl.when(second)
            def _():
                text_whole(there.at[TEXT, NEAR], near_text, False)

        return carry

    lax.fori_loop(0, parts, steps, 0)

    tail(parts - 1).wait_send()
    whole.wait_send()
    pos_link.wait_send()
    pos_near(pos_ref).wait_send()

    def drain(c, carry):
        pass_on(c).wait_send()
        return carry

    lax.fori_loop(0, parts, drain, 0)
    tail(parts - 1).wait_recv()

    @pl.when(first)
    def _():
        text_part(there.at[TEXT, FAR], far_text, parts - 1, last=True)
        losses()

    @pl.when(second)
    def _():
        image_part(there.at[IMAGE, FAR], places.at[FAR], parts - 1, last=True)


def shards(images, texts, positive, log_scale, bias):
    rows, width = images.shape
    parts = rows // PART
    two = pltpu.VMEM((2, rows, width), jnp.bfloat16)
    column = pltpu.VMEM((rows, 128), jnp.float32)
    sems = pltpu.SemaphoreType.DMA((parts,))
    one = pltpu.SemaphoreType.DMA((1,))
    pair = pltpu.SemaphoreType.DMA((2,))
    vmem = pl.BlockSpec(memory_space=pltpu.VMEM)
    hbm = pl.BlockSpec(memory_space=pltpu.HBM)
    loss, grad_x, grad_y = pl.pallas_call(
        kernel,
        out_shape=(
            jax.ShapeDtypeStruct((rows // 128, 128), jnp.float32),
            pltpu.VMEM((rows, width), jnp.float32),
            pltpu.VMEM((rows, width), jnp.float32),
        ),
        in_specs=[hbm] * 5,
        out_specs=(vmem, vmem, vmem),
        scratch_shapes=[
            pltpu.SMEM((1,), jnp.float32),
            pltpu.SMEM((1,), jnp.float32),
            pltpu.VMEM((rows // 128, 128), jnp.int32),
            two,
            two,
            pltpu.VMEM((2, rows, 128), jnp.float32),
            pltpu.VMEM((2, 2, rows, width), jnp.bfloat16),
            pltpu.VMEM((2, rows // 128, 128), jnp.int32),
            column,
            column,
            pltpu.SemaphoreType.DMA((5,)),
            sems, sems, sems, sems, sems, sems, one, one, pair, pair,
        ],
        compiler_params=pltpu.CompilerParams(
            collective_id=0, has_side_effects=True, vmem_limit_bytes=56 * 2**20),
    )(log_scale, bias, positive.reshape(rows // 128, 128), images, texts)
    return (loss.reshape(rows), grad_x, grad_y)


def solution(mesh):
    in_specs = (
        P(("rep", "blk"), None),
        P(("rep", "blk"), None),
        P(("rep", "blk")),
        P("rep"),
        P("rep"),
    )
    out_specs = (P(("rep", "blk")), P(("rep", "blk"), None), P(("rep", "blk"), None))
    return jax.shard_map(shards, mesh=mesh, in_specs=in_specs, out_specs=out_specs, check_vma=False)
```

```python
import functools

import jax
import jax.numpy as jnp
from jax import lax
from jax.experimental import pallas as pl
from jax.experimental.pallas import tpu as pltpu
from jax.sharding import PartitionSpec as P

PART = 128
TILE = 256
LAST_TILE = 256
IN_FLIGHT = 3
MESH = pl.DeviceIdType.MESH
IMAGE, TEXT = 0, 1
FAR, NEAR = 0, 1


def at_rows(start, size):
    return pl.ds(pl.multiple_of(start, size), size)


def kernel(
    scale_hbm, bias_hbm, pos_hbm, img_ref, txt_ref,
    loss_ref, gx_ref, gy_ref,
    scale_ref, bias_ref, pos_ref, raw, low, inv, there, places, posb, loss_acc,
    load_sem, lead_s, lead_r, tail_s, tail_r, pass_s, pass_r, whole_s, whole_r, pos_s, pos_r,
):
    _, rows, width = raw.shape
    parts = rows // PART
    tiles = rows // TILE
    n = lax.axis_size("blk")
    me = lax.axis_index("blk")
    core = lax.rem(me, 2)
    other = 1 - core
    ahead = lax.rem(me + 2, n)
    behind = lax.rem(me + n - 2, n)
    partner = me + 1 - 2 * core
    first = core == 0
    second = core == 1

    barrier = pltpu.get_barrier_semaphore()
    for device in (ahead, behind, partner):
        pl.semaphore_signal(barrier, inc=1, device_id={"blk": device}, device_id_type=MESH)

    loads = [
        pltpu.make_async_copy(img_ref, raw.at[IMAGE], load_sem.at[0]),
        pltpu.make_async_copy(txt_ref, raw.at[TEXT], load_sem.at[1]),
        pltpu.make_async_copy(pos_hbm, pos_ref, load_sem.at[2]),
        pltpu.make_async_copy(scale_hbm, scale_ref, load_sem.at[3]),
        pltpu.make_async_copy(bias_hbm, bias_ref, load_sem.at[4]),
    ]
    for load in loads:
        load.start()

    def remote(source, target, sent, got, device):
        return pltpu.make_async_remote_copy(
            src_ref=source, dst_ref=target, send_sem=sent, recv_sem=got,
            device_id={"blk": device}, device_id_type=MESH)

    def lead(c):
        r = at_rows(c * PART, PART)
        return remote(low.at[core, r], there.at[core, FAR, r], lead_s.at[c], lead_r.at[c],
                      jnp.where(first, behind, ahead))

    def tail(c):
        r = at_rows(c * PART, PART)
        return remote(low.at[other, r], there.at[other, FAR, r], tail_s.at[c], tail_r.at[c],
                      jnp.where(first, ahead, behind))

    def pass_on(c):
        r = at_rows(c * PART, PART)
        return remote(there.at[core, FAR, r], there.at[core, NEAR, r], pass_s.at[c], pass_r.at[c], partner)

    whole = remote(low.at[other], there.at[other, NEAR], whole_s.at[0], whole_r.at[0], partner)
    pos_link = remote(pos_ref, places.at[FAR], pos_s.at[0], pos_r.at[0], behind)

    def pos_near(source):
        return remote(source, places.at[NEAR], pos_s.at[1], pos_r.at[1], partner)

    def normalize(kind):
        def step(c, carry):
            r = at_rows(c * PART, PART)
            wide = raw[kind, r, :].astype(jnp.float32)
            inverse = lax.rsqrt(jnp.sum(wide * wide, axis=-1, keepdims=True) + 1e-06)
            inv[kind, r, :] = jnp.broadcast_to(inverse, (PART, 128))
            low[kind, r, :] = (wide * inverse).astype(jnp.bfloat16)
            return carry

        lax.fori_loop(0, parts, step, 0)

    for load in loads:
        load.wait()
    normalize(core)
    pl.semaphore_wait(barrier, 3)
    def start(p):
        is_tail = jnp.logical_or(p == 2 * parts - 1, jnp.logical_and(p > 0, lax.rem(p, 2) == 0))

        @pl.when(jnp.logical_and(p < 2 * parts, is_tail))
        def _():
            tail(lax.div(p - 1, 2)).start()

        @pl.when(jnp.logical_and(p < 2 * parts, jnp.logical_not(is_tail)))
        def _():
            lead(lax.div(p + 1, 2)).start()

    def fill(p, carry):
        start(p)
        return carry

    pos_link.start()

    @pl.when(second)
    def _():
        pos_near(pos_ref).start()

    lax.fori_loop(0, 2, fill, 0)
    normalize(other)
    whole.start()
    lax.fori_loop(2, IN_FLIGHT, fill, 0)

    scale = jnp.exp(jnp.full((8, 128), scale_ref[0], jnp.float32))[0:1, 0:1]
    bias = bias_ref[0]

    def spread(c, carry):
        row = pos_ref[pl.ds(c, 1), :].astype(jnp.float32)
        posb[at_rows(c * 128, 128), :] = jnp.broadcast_to(row, (128, 128)).T
        return carry

    lax.fori_loop(0, rows // 128, spread, 0)

    def logits_of(own, block):
        dots = lax.dot_general(own, block, (((1,), (1,)), ((), ())), preferred_element_type=jnp.float32)
        return scale * dots + bias

    def text_terms(at, block, target, wide):
        scaled = logits_of(low[IMAGE, at, :], block)
        match = jnp.concatenate([posb[at, :]] * (wide // 128), axis=1) == target
        z = jnp.where(match, -scaled, scaled)
        e = jnp.exp(-jnp.abs(z))
        term = jnp.maximum(z, 0.0) + jnp.log1p(e)
        s = jnp.where(z >= 0, 1.0, e) / (1.0 + e)
        coefficient = jnp.where(match, -s, s).astype(jnp.bfloat16)
        loss = functools.reduce(jnp.add, [term[:, g:g + 128] for g in range(0, wide, 128)])
        return loss, jnp.dot(coefficient, block, preferred_element_type=jnp.float32)

    def image_terms(at, start, size, block, pos_row):
        scaled = logits_of(low[TEXT, at, :], block)
        subs = lax.broadcasted_iota(jnp.int32, scaled.shape, 0)
        match = pos_row == me * rows + start + subs
        z = jnp.where(match, -scaled, scaled)
        s = 1.0 / (1.0 + jnp.exp(-z))
        coefficient = jnp.where(match, -s, s).astype(jnp.bfloat16)
        return jnp.dot(coefficient, block, preferred_element_type=jnp.float32)

    def targets(source, start, size, wide):
        lanes = lax.broadcasted_iota(jnp.int32, (size, wide), 1)
        return (source * rows + start + lanes).astype(jnp.float32)

    def text_whole(block, source, fresh):
        def step(t, carry):
            at = at_rows(t * TILE, TILE)
            loss, grad = text_terms(at, block[...], targets(source, 0, TILE, rows), rows)
            loss_acc[at, :] = loss if fresh else loss_acc[at, :] + loss
            gx_ref[at, :] = grad if fresh else gx_ref[at, :] + grad
            return carry

        lax.fori_loop(0, tiles, step, 0)

    def image_whole(block, positions, fresh):
        pos_row = jnp.concatenate([positions[g:g + 1, :] for g in range(rows // 128)], axis=1)

        def step(t, carry):
            at = at_rows(t * TILE, TILE)
            grad = image_terms(at, t * TILE, TILE, block[...], pos_row)
            gy_ref[at, :] = grad if fresh else gy_ref[at, :] + grad
            return carry

        lax.fori_loop(0, tiles, step, 0)

    def project(grad, kind, at):
        inverse = inv[kind, at, :][:, 0:1]
        unit = raw[kind, at, :].astype(jnp.float32) * inverse
        grad = grad * scale
        return (grad - unit * jnp.sum(unit * grad, axis=-1, keepdims=True)) * inverse

    def text_part(block, source, c, last=False):
        size = LAST_TILE if last else TILE
        chunk = block[at_rows(c * PART, PART), :]
        for t in range(rows // size):
            at = pl.ds(t * size, size)
            loss, grad = text_terms(at, chunk, targets(source, c * PART, size, PART), PART)
            loss_acc[at, :] += loss
            grad = gx_ref[at, :] + grad
            gx_ref[at, :] = project(grad, IMAGE, at) if last else grad

    def image_part(block, positions, c, last=False):
        size = LAST_TILE if last else TILE
        chunk = block[at_rows(c * PART, PART), :]
        pos_row = positions[pl.ds(c, 1), :]
        for t in range(rows // size):
            at = pl.ds(t * size, size)
            grad = gy_ref[at, :] + image_terms(at, t * size, size, chunk, pos_row)
            gy_ref[at, :] = project(grad, TEXT, at) if last else grad

    def finish(acc, kind):
        def step(t, carry):
            at = at_rows(t * TILE, TILE)
            acc[at, :] = project(acc[at, :], kind, at)
            return carry

        lax.fori_loop(0, tiles, step, 0)

    def losses():
        for c in range(rows // 128):
            total = jnp.sum(loss_acc[c * 128:(c + 1) * 128, :].T, axis=0, keepdims=True)
            loss_ref[c:c + 1, :] = total / rows

    near_text = lax.rem(me + n - 1, n)
    far_text = lax.rem(me + n - 2, n)

    text_whole(low.at[TEXT], me, True)
    image_whole(low.at[IMAGE], pos_ref, True)
    def steps(c, carry):
        lead(c).wait_send()

        start(jnp.where(c == 0, 0, 2 * c - 1) + IN_FLIGHT)
        lead(c).wait_recv()

        @pl.when(c == 0)
        def _():
            pos_link.wait_recv()

            @pl.when(first)
            def _():
                pos_near(places.at[FAR]).start()

            pos_near(pos_ref).wait_recv()

        pass_on(c).start()
        pass_on(c).wait_recv()
        image_part(there.at[IMAGE, core], places.at[core], c)
        text_part(there.at[TEXT, other], jnp.where(first, near_text, far_text), c)

        @pl.when(c > 0)
        def _():
            tail(c - 1).wait_send()
            start(2 * c + IN_FLIGHT)

        @pl.when(jnp.logical_and(c == parts - 1, first))
        def _():
            finish(gy_ref, TEXT)

        @pl.when(jnp.logical_and(c == parts - 1, second))
        def _():
            finish(gx_ref, IMAGE)
            losses()

        @pl.when(c > 0)
        def _():
            tail(c - 1).wait_recv()

            @pl.when(first)
            def _():
                text_part(there.at[TEXT, FAR], far_text, c - 1)

            @pl.when(second)
            def _():
                image_part(there.at[IMAGE, FAR], places.at[FAR], c - 1)

        @pl.when(c == 1)
        def _():
            whole.wait_recv()

            @pl.when(first)
            def _():
                image_whole(there.at[IMAGE, NEAR], places.at[NEAR], False)

            @pl.when(second)
            def _():
                text_whole(there.at[TEXT, NEAR], near_text, False)

        return carry

    lax.fori_loop(0, parts, steps, 0)

    tail(parts - 1).wait_send()
    whole.wait_send()
    pos_link.wait_send()
    pos_near(pos_ref).wait_send()

    def drain(c, carry):
        pass_on(c).wait_send()
        return carry

    lax.fori_loop(0, parts, drain, 0)
    tail(parts - 1).wait_recv()

    @pl.when(first)
    def _():
        text_part(there.at[TEXT, FAR], far_text, parts - 1, last=True)
        losses()

    @pl.when(second)
    def _():
        image_part(there.at[IMAGE, FAR], places.at[FAR], parts - 1, last=True)


def shards(images, texts, positive, log_scale, bias):
    rows, width = images.shape
    parts = rows // PART
    two = pltpu.VMEM((2, rows, width), jnp.bfloat16)
    column = pltpu.VMEM((rows, 128), jnp.float32)
    sems = pltpu.SemaphoreType.DMA((parts,))
    one = pltpu.SemaphoreType.DMA((1,))
    pair = pltpu.SemaphoreType.DMA((2,))
    vmem = pl.BlockSpec(memory_space=pltpu.VMEM)
    hbm = pl.BlockSpec(memory_space=pltpu.HBM)
    loss, grad_x, grad_y = pl.pallas_call(
        kernel,
        out_shape=(
            jax.ShapeDtypeStruct((rows // 128, 128), jnp.float32),
            pltpu.VMEM((rows, width), jnp.float32),
            pltpu.VMEM((rows, width), jnp.float32),
        ),
        in_specs=[hbm] * 5,
        out_specs=(vmem, vmem, vmem),
        scratch_shapes=[
            pltpu.SMEM((1,), jnp.float32),
            pltpu.SMEM((1,), jnp.float32),
            pltpu.VMEM((rows // 128, 128), jnp.int32),
            two,
            two,
            pltpu.VMEM((2, rows, 128), jnp.float32),
            pltpu.VMEM((2, 2, rows, width), jnp.bfloat16),
            pltpu.VMEM((2, rows // 128, 128), jnp.int32),
            column,
            column,
            pltpu.SemaphoreType.DMA((5,)),
            sems, sems, sems, sems, sems, sems, one, one, pair, pair,
        ],
        compiler_params=pltpu.CompilerParams(
            collective_id=0, has_side_effects=True, vmem_limit_bytes=56 * 2**20),
    )(log_scale, bias, positive.reshape(rows // 128, 128), images, texts)
    return (loss.reshape(rows), grad_x, grad_y)


def solution(mesh):
    in_specs = (
        P(("rep", "blk"), None),
        P(("rep", "blk"), None),
        P(("rep", "blk")),
        P("rep"),
        P("rep"),
    )
    out_specs = (P(("rep", "blk")), P(("rep", "blk"), None), P(("rep", "blk"), None))
    return jax.shard_map(shards, mesh=mesh, in_specs=in_specs, out_specs=out_specs, check_vma=False)
```

```python
import functools

import jax
import jax.numpy as jnp
from jax import lax
from jax.experimental import pallas as pl
from jax.experimental.pallas import tpu as pltpu
from jax.sharding import PartitionSpec as P

PART = 128
TILE = 384
LAST_TILE = 384
IN_FLIGHT = 3
MESH = pl.DeviceIdType.MESH
IMAGE, TEXT = 0, 1
FAR, NEAR = 0, 1


def at_rows(start, size):
    return pl.ds(pl.multiple_of(start, size), size)


def kernel(
    scale_hbm, bias_hbm, pos_hbm, img_ref, txt_ref,
    loss_ref, gx_ref, gy_ref,
    scale_ref, bias_ref, pos_ref, raw, low, inv, there, places, posb, loss_acc,
    load_sem, lead_s, lead_r, tail_s, tail_r, pass_s, pass_r, whole_s, whole_r, pos_s, pos_r,
):
    _, rows, width = raw.shape
    parts = rows // PART
    tiles = rows // TILE
    n = lax.axis_size("blk")
    me = lax.axis_index("blk")
    core = lax.rem(me, 2)
    other = 1 - core
    ahead = lax.rem(me + 2, n)
    behind = lax.rem(me + n - 2, n)
    partner = me + 1 - 2 * core
    first = core == 0
    second = core == 1

    barrier = pltpu.get_barrier_semaphore()
    for device in (ahead, behind, partner):
        pl.semaphore_signal(barrier, inc=1, device_id={"blk": device}, device_id_type=MESH)

    loads = [
        pltpu.make_async_copy(img_ref, raw.at[IMAGE], load_sem.at[0]),
        pltpu.make_async_copy(txt_ref, raw.at[TEXT], load_sem.at[1]),
        pltpu.make_async_copy(pos_hbm, pos_ref, load_sem.at[2]),
        pltpu.make_async_copy(scale_hbm, scale_ref, load_sem.at[3]),
        pltpu.make_async_copy(bias_hbm, bias_ref, load_sem.at[4]),
    ]
    for load in loads:
        load.start()

    def remote(source, target, sent, got, device):
        return pltpu.make_async_remote_copy(
            src_ref=source, dst_ref=target, send_sem=sent, recv_sem=got,
            device_id={"blk": device}, device_id_type=MESH)

    def lead(c):
        r = at_rows(c * PART, PART)
        return remote(low.at[core, r], there.at[core, FAR, r], lead_s.at[c], lead_r.at[c],
                      jnp.where(first, behind, ahead))

    def tail(c):
        r = at_rows(c * PART, PART)
        return remote(low.at[other, r], there.at[other, FAR, r], tail_s.at[c], tail_r.at[c],
                      jnp.where(first, ahead, behind))

    def pass_on(c):
        r = at_rows(c * PART, PART)
        return remote(there.at[core, FAR, r], there.at[core, NEAR, r], pass_s.at[c], pass_r.at[c], partner)

    whole = remote(low.at[other], there.at[other, NEAR], whole_s.at[0], whole_r.at[0], partner)
    pos_link = remote(pos_ref, places.at[FAR], pos_s.at[0], pos_r.at[0], behind)

    def pos_near(source):
        return remote(source, places.at[NEAR], pos_s.at[1], pos_r.at[1], partner)

    def normalize(kind):
        def step(c, carry):
            r = at_rows(c * PART, PART)
            wide = raw[kind, r, :].astype(jnp.float32)
            inverse = lax.rsqrt(jnp.sum(wide * wide, axis=-1, keepdims=True) + 1e-06)
            inv[kind, r, :] = jnp.broadcast_to(inverse, (PART, 128))
            low[kind, r, :] = (wide * inverse).astype(jnp.bfloat16)
            return carry

        lax.fori_loop(0, parts, step, 0)

    for load in loads:
        load.wait()
    normalize(core)
    pl.semaphore_wait(barrier, 3)
    def start(p):
        is_tail = jnp.logical_or(p == 2 * parts - 1, jnp.logical_and(p > 0, lax.rem(p, 2) == 0))

        @pl.when(jnp.logical_and(p < 2 * parts, is_tail))
        def _():
            tail(lax.div(p - 1, 2)).start()

        @pl.when(jnp.logical_and(p < 2 * parts, jnp.logical_not(is_tail)))
        def _():
            lead(lax.div(p + 1, 2)).start()

    def fill(p, carry):
        start(p)
        return carry

    pos_link.start()

    @pl.when(second)
    def _():
        pos_near(pos_ref).start()

    lax.fori_loop(0, 2, fill, 0)
    normalize(other)
    whole.start()
    lax.fori_loop(2, IN_FLIGHT, fill, 0)

    scale = jnp.exp(jnp.full((8, 128), scale_ref[0], jnp.float32))[0:1, 0:1]
    bias = bias_ref[0]

    def spread(c, carry):
        row = pos_ref[pl.ds(c, 1), :].astype(jnp.float32)
        posb[at_rows(c * 128, 128), :] = jnp.broadcast_to(row, (128, 128)).T
        return carry

    lax.fori_loop(0, rows // 128, spread, 0)

    def logits_of(own, block):
        dots = lax.dot_general(own, block, (((1,), (1,)), ((), ())), preferred_element_type=jnp.float32)
        return scale * dots + bias

    def text_terms(at, block, target, wide):
        scaled = logits_of(low[IMAGE, at, :], block)
        match = jnp.concatenate([posb[at, :]] * (wide // 128), axis=1) == target
        z = jnp.where(match, -scaled, scaled)
        e = jnp.exp(-jnp.abs(z))
        term = jnp.maximum(z, 0.0) + jnp.log1p(e)
        s = jnp.where(z >= 0, 1.0, e) / (1.0 + e)
        coefficient = jnp.where(match, -s, s).astype(jnp.bfloat16)
        loss = functools.reduce(jnp.add, [term[:, g:g + 128] for g in range(0, wide, 128)])
        return loss, jnp.dot(coefficient, block, preferred_element_type=jnp.float32)

    def image_terms(at, start, size, block, pos_row):
        scaled = logits_of(low[TEXT, at, :], block)
        subs = lax.broadcasted_iota(jnp.int32, scaled.shape, 0)
        match = pos_row == me * rows + start + subs
        z = jnp.where(match, -scaled, scaled)
        s = 1.0 / (1.0 + jnp.exp(-z))
        coefficient = jnp.where(match, -s, s).astype(jnp.bfloat16)
        return jnp.dot(coefficient, block, preferred_element_type=jnp.float32)

    def targets(source, start, size, wide):
        lanes = lax.broadcasted_iota(jnp.int32, (size, wide), 1)
        return (source * rows + start + lanes).astype(jnp.float32)

    def text_whole(block, source, fresh):
        def step(t, carry):
            at = at_rows(t * TILE, TILE)
            loss, grad = text_terms(at, block[...], targets(source, 0, TILE, rows), rows)
            loss_acc[at, :] = loss if fresh else loss_acc[at, :] + loss
            gx_ref[at, :] = grad if fresh else gx_ref[at, :] + grad
            return carry

        lax.fori_loop(0, tiles, step, 0)

    def image_whole(block, positions, fresh):
        pos_row = jnp.concatenate([positions[g:g + 1, :] for g in range(rows // 128)], axis=1)

        def step(t, carry):
            at = at_rows(t * TILE, TILE)
            grad = image_terms(at, t * TILE, TILE, block[...], pos_row)
            gy_ref[at, :] = grad if fresh else gy_ref[at, :] + grad
            return carry

        lax.fori_loop(0, tiles, step, 0)

    def project(grad, kind, at):
        inverse = inv[kind, at, :][:, 0:1]
        unit = raw[kind, at, :].astype(jnp.float32) * inverse
        grad = grad * scale
        return (grad - unit * jnp.sum(unit * grad, axis=-1, keepdims=True)) * inverse

    def text_part(block, source, c, last=False):
        size = LAST_TILE if last else TILE
        chunk = block[at_rows(c * PART, PART), :]
        for t in range(rows // size):
            at = pl.ds(t * size, size)
            loss, grad = text_terms(at, chunk, targets(source, c * PART, size, PART), PART)
            loss_acc[at, :] += loss
            grad = gx_ref[at, :] + grad
            gx_ref[at, :] = project(grad, IMAGE, at) if last else grad

    def image_part(block, positions, c, last=False):
        size = LAST_TILE if last else TILE
        chunk = block[at_rows(c * PART, PART), :]
        pos_row = positions[pl.ds(c, 1), :]
        for t in range(rows // size):
            at = pl.ds(t * size, size)
            grad = gy_ref[at, :] + image_terms(at, t * size, size, chunk, pos_row)
            gy_ref[at, :] = project(grad, TEXT, at) if last else grad

    def finish(acc, kind):
        def step(t, carry):
            at = at_rows(t * TILE, TILE)
            acc[at, :] = project(acc[at, :], kind, at)
            return carry

        lax.fori_loop(0, tiles, step, 0)

    def losses():
        for c in range(rows // 128):
            total = jnp.sum(loss_acc[c * 128:(c + 1) * 128, :].T, axis=0, keepdims=True)
            loss_ref[c:c + 1, :] = total / rows

    near_text = lax.rem(me + n - 1, n)
    far_text = lax.rem(me + n - 2, n)

    text_whole(low.at[TEXT], me, True)
    image_whole(low.at[IMAGE], pos_ref, True)
    def steps(c, carry):
        lead(c).wait_send()

        start(jnp.where(c == 0, 0, 2 * c - 1) + IN_FLIGHT)
        lead(c).wait_recv()

        @pl.when(c == 0)
        def _():
            pos_link.wait_recv()

            @pl.when(first)
            def _():
                pos_near(places.at[FAR]).start()

            pos_near(pos_ref).wait_recv()

        pass_on(c).start()
        pass_on(c).wait_recv()
        image_part(there.at[IMAGE, core], places.at[core], c)
        text_part(there.at[TEXT, other], jnp.where(first, near_text, far_text), c)

        @pl.when(c > 0)
        def _():
            tail(c - 1).wait_send()
            start(2 * c + IN_FLIGHT)

        @pl.when(jnp.logical_and(c == parts - 1, first))
        def _():
            finish(gy_ref, TEXT)

        @pl.when(jnp.logical_and(c == parts - 1, second))
        def _():
            finish(gx_ref, IMAGE)
            losses()

        @pl.when(c > 0)
        def _():
            tail(c - 1).wait_recv()

            @pl.when(first)
            def _():
                text_part(there.at[TEXT, FAR], far_text, c - 1)

            @pl.when(second)
            def _():
                image_part(there.at[IMAGE, FAR], places.at[FAR], c - 1)

        @pl.when(c == 1)
        def _():
            whole.wait_recv()

            @pl.when(first)
            def _():
                image_whole(there.at[IMAGE, NEAR], places.at[NEAR], False)

            @pl.when(second)
            def _():
                text_whole(there.at[TEXT, NEAR], near_text, False)

        return carry

    lax.fori_loop(0, parts, steps, 0)

    tail(parts - 1).wait_send()
    whole.wait_send()
    pos_link.wait_send()
    pos_near(pos_ref).wait_send()

    def drain(c, carry):
        pass_on(c).wait_send()
        return carry

    lax.fori_loop(0, parts, drain, 0)
    tail(parts - 1).wait_recv()

    @pl.when(first)
    def _():
        text_part(there.at[TEXT, FAR], far_text, parts - 1, last=True)
        losses()

    @pl.when(second)
    def _():
        image_part(there.at[IMAGE, FAR], places.at[FAR], parts - 1, last=True)


def shards(images, texts, positive, log_scale, bias):
    rows, width = images.shape
    parts = rows // PART
    two = pltpu.VMEM((2, rows, width), jnp.bfloat16)
    column = pltpu.VMEM((rows, 128), jnp.float32)
    sems = pltpu.SemaphoreType.DMA((parts,))
    one = pltpu.SemaphoreType.DMA((1,))
    pair = pltpu.SemaphoreType.DMA((2,))
    vmem = pl.BlockSpec(memory_space=pltpu.VMEM)
    hbm = pl.BlockSpec(memory_space=pltpu.HBM)
    loss, grad_x, grad_y = pl.pallas_call(
        kernel,
        out_shape=(
            jax.ShapeDtypeStruct((rows // 128, 128), jnp.float32),
            pltpu.VMEM((rows, width), jnp.float32),
            pltpu.VMEM((rows, width), jnp.float32),
        ),
        in_specs=[hbm] * 5,
        out_specs=(vmem, vmem, vmem),
        scratch_shapes=[
            pltpu.SMEM((1,), jnp.float32),
            pltpu.SMEM((1,), jnp.float32),
            pltpu.VMEM((rows // 128, 128), jnp.int32),
            two,
            two,
            pltpu.VMEM((2, rows, 128), jnp.float32),
            pltpu.VMEM((2, 2, rows, width), jnp.bfloat16),
            pltpu.VMEM((2, rows // 128, 128), jnp.int32),
            column,
            column,
            pltpu.SemaphoreType.DMA((5,)),
            sems, sems, sems, sems, sems, sems, one, one, pair, pair,
        ],
        compiler_params=pltpu.CompilerParams(
            collective_id=0, has_side_effects=True, vmem_limit_bytes=56 * 2**20),
    )(log_scale, bias, positive.reshape(rows // 128, 128), images, texts)
    return (loss.reshape(rows), grad_x, grad_y)


def solution(mesh):
    in_specs = (
        P(("rep", "blk"), None),
        P(("rep", "blk"), None),
        P(("rep", "blk")),
        P("rep"),
        P("rep"),
    )
    out_specs = (P(("rep", "blk")), P(("rep", "blk"), None), P(("rep", "blk"), None))
    return jax.shard_map(shards, mesh=mesh, in_specs=in_specs, out_specs=out_specs, check_vma=False)
```
